32 devices in a mesh: grp: 2 (over x), leaf: 16 (over z, y, core).
Axes of the slice: x: 2, y: 2, z: 4, core: 2. Of those that a mesh axis runs over, the one named last changes fastest.
Arguments:
- rhs: float32 [32, 256, 128], P(None, ('grp', 'leaf')), parts along dimension 1, may hold values from -6 to 6
- near_blocks: float32 [256, 8, 128, 128], P(('grp', 'leaf')), parts along dimension 0
- near_nbrs: int32 [256, 8], P(('grp', 'leaf')), parts along dimension 0, may hold values from 0 to 127, as said below
- row_basis: float32 [256, 128, 16], P(('grp', 'leaf')), parts along dimension 0, may hold values from -0.5 to 0.5
- col_basis: float32 [256, 128, 16], P(('grp', 'leaf')), parts along dimension 0, may hold values from -0.5 to 0.5
- couplings: float32 [4096, 16, 16], P(('grp', 'leaf')), parts along dimension 0, may hold values from -0.375 to 0.375
- far_owner: int32 [4096, 1], P(('grp', 'leaf')), parts along dimension 0, may hold values from 0 to 15; in each aligned block of 128 rows (0 to 127, 128 to 255, ...) at most 16 rows name the same one
- far_slot: int32 [4096], P(('grp', 'leaf')), parts along dimension 0, may hold values from 0 to 7
- leaf_perm: int32 [256, 128], P(('grp', 'leaf')), parts along dimension 0, may hold values from 0 to 127, each once within a row
- leaf_size: int32 [256], P(('grp', 'leaf')), parts along dimension 0, may hold values from 64 to 128, as said below
Outputs:
- solution: float32 [32, 256, 128], P(None, ('grp', 'leaf')), parts along dimension 1
The draws below stay inside these ranges and needn't reach their ends.
There are 2 independent parts, one for each index of `grp`. The reference program is written for one: setup_inputs(seed, part) draws one part's arguments, and reference() takes and returns one part's arrays. A program takes and returns all parts, laid end to end along the dimension named above; each array names one. Nothing has to cross between parts.
Inputs may be any that keep to these rules, and one draw needn't show every extreme that they name: `near_nbrs`: entry 0 of a leaf's list is the leaf itself, entry 1 lies exactly 8 leaves away, and every entry lies within 8 leaves of the leaf. `far_owner`: among the far blocks of one device at most 16 name any one owner. `leaf_size`: the first leaf of every device is full.
All inputs are finite; a program needn't handle non-finite values.
Results may differ from the reference program's by a relative error of at most 0.0003.
Values sent between devices are 32-bit elements; how exact they have to be, the bound alone decides.
A program may use at most 64 MiB of HBM per device.

```python
import math
import jax
import jax.numpy as jnp
import numpy as np
from jax import lax

R = 32
M = 128
K = 16
NB = 8
FAR_LEAF = 16
ITERS = 3
LEAVES_DEV = 8
LEAVES = 128
FAR_DEV = 128
FAR = 2048
CAP = 16
N_LEAF = 16


def draw_near_blocks(key, part):
    key = jax.random.fold_in(key, 11)
    block_shape = (LEAVES, NB, M, M)
    spread = (0.5 / (NB * M)) ** 0.5
    noise = jax.random.normal(key, block_shape, jnp.float32) * spread
    slot_index = lax.broadcasted_iota(jnp.int32, block_shape, 1)
    row_index = lax.broadcasted_iota(jnp.int32, block_shape, 2)
    col_index = lax.broadcasted_iota(jnp.int32, block_shape, 3)
    return noise + jnp.where((slot_index == 0) & (row_index == col_index), 3.0, 0.0)


def draw_near_nbrs(key, part):
    key = jax.random.fold_in(key, 12)
    leaf_index = lax.broadcasted_iota(jnp.int32, (LEAVES, NB), 0)
    slot_index = lax.broadcasted_iota(jnp.int32, (LEAVES, NB), 1)
    offsets = jax.random.randint(key, (LEAVES, NB), -LEAVES_DEV, LEAVES_DEV + 1)
    reach = jnp.where(leaf_index >= LEAVES_DEV, leaf_index - LEAVES_DEV, leaf_index + LEAVES_DEV)
    chosen = jnp.clip(leaf_index + offsets, 0, LEAVES - 1)
    return jnp.where(slot_index == 0, leaf_index, jnp.where(slot_index == 1, reach, chosen)).astype(jnp.int32)


def draw_leaf_size(key, part):
    key = jax.random.fold_in(key, 13)
    sizes = jax.random.randint(key, (LEAVES,), M // 2, M + 1)
    leaf_index = lax.broadcasted_iota(jnp.int32, (LEAVES,), 0)
    return jnp.where(leaf_index % LEAVES_DEV == 0, M, sizes).astype(jnp.int32)


def plant(array, rng, low, largest):
    longest = array.shape.index(max(array.shape))
    spots = []
    for shift in (0, 1):
        where = [jax.random.randint(jax.random.fold_in(rng, axis), (), 0, length) for axis, length in enumerate(array.shape)]
        where[longest] = (where[longest] + shift) % array.shape[longest]
        spots.append(tuple(where))
    return array.at[spots[0]].set(low).at[spots[1]].set(largest)


def steps_of(key, shape, split, least, largest):
    def one(axis_at, parts):
        draws = jax.random.uniform(jax.random.fold_in(jax.random.fold_in(key, 6), axis_at), (parts,), jnp.float32, least / len(split), largest / len(split))
        return jnp.repeat(jnp.exp(draws), shape[axis_at] // parts).reshape((-1,) + (1,) * (len(shape) - axis_at - 1))

    loudness = one(*split[0])
    for cut in split[1:]:
        loudness = loudness * one(*cut)
    return loudness


def shared_out(rng, own, number, rows, number_of, top, limit, slope):
    ranking = jax.random.permutation(rng, number_of)
    crowded, common = portions_of(number_of, rows * top, limit, slope, True), portions_of(number_of, rows * top, limit, slope, False)
    places = jnp.arange(number_of)

    def named(tallies, offset_by):
        used = int((tallies > 0).sum())
        fixed = max(1, used // 4)
        passed = fixed + (places - fixed + offset_by * (used - fixed)) % max(1, number_of - fixed)
        return jnp.zeros((number_of,), jnp.int32).at[ranking[jnp.where(places < fixed, places, passed)]].set(jnp.asarray(tallies, jnp.int32))

    tallies = jnp.where(number % 4 == 0, named(crowded, number // 4), named(common, number - number // 4 - 1))
    mixed = jax.random.permutation(jax.random.fold_in(own, 3), number_of)
    source_of, taker = mixed[0:number_of // 2 * 2:2], mixed[1:number_of // 2 * 2:2]
    room = jnp.minimum(tallies[source_of] - 1, limit - tallies[taker]) // 2
    room = jnp.where((source_of == ranking[0]) | (taker == ranking[0]) | (tallies[taker] == 0), 0, jnp.maximum(room, 0))
    passed = jax.random.randint(jax.random.fold_in(own, 4), (number_of // 2,), 0, 1 << 20) % (room + 1)
    tallies = tallies.at[source_of].add(-passed).at[taker].add(passed)
    members = jnp.searchsorted(jnp.cumsum(tallies), jnp.arange(rows * top), side="right").astype(jnp.int32)
    grid = members.reshape(top, rows).T
    grid = grid[jax.random.permutation(jax.random.fold_in(own, 1), rows)]
    offset_by = jax.random.randint(jax.random.fold_in(own, 2), (rows, 1), 0, top)
    return jnp.take_along_axis(grid, (jnp.arange(top)[None, :] + offset_by) % top, axis=1)


def portions_of(amount, total, limit, skew, full):
    weights = [(1 << 20) // math.isqrt(rank ** skew) + 1 for rank in range(1, amount + 1)]
    largest = limit if full else min(limit, max(-(-total // amount), total * weights[0] // sum(weights)))
    least = 1 if total - largest >= amount - 1 else 0
    counts, surplus = [largest] + [least] * (amount - 1), total - largest - least * (amount - 1)
    while surplus > 0:
        free = [i for i in range(1, amount) if counts[i] < largest] or [i for i in range(1, amount) if counts[i] < limit]
        mass, remaining = sum([weights[i] for i in free]), surplus
        for i in free:
            more = min(limit - counts[i], max(1, remaining * weights[i] // mass), surplus)
            counts[i] = counts[i] + more
            surplus = surplus - more
    return np.array(counts)


def bell_draw(key, shape, scale, most, split=(), kind=jnp.bfloat16):
    drawn = scale * jax.random.normal(key, shape, jnp.float32)
    if split:
        drawn = drawn * steps_of(key, shape, split, -0.22, 0.18)
    return jnp.clip(drawn, -most, most).astype(kind)


def setup_inputs(seed: int = 0, part: int = 0) -> dict:
    seeds = jax.random.split(jax.random.key(seed), 11)
    part_keys = jax.random.split(jax.random.fold_in(seeds[10], part), 11)
    rhs = bell_draw(part_keys[0], (R, LEAVES, M), 1.0, 6.0, ((1, 16),), jnp.float32)
    near_blocks = draw_near_blocks(jax.random.fold_in(jax.random.fold_in(seeds[10], part), 71), part)
    near_nbrs = draw_near_nbrs(jax.random.fold_in(jax.random.fold_in(seeds[10], part), 71), part)
    row_basis = bell_draw(part_keys[3], (LEAVES, M, K), M ** -0.5, 0.5, ((0, 16),), jnp.float32)
    col_basis = bell_draw(part_keys[4], (LEAVES, M, K), M ** -0.5, 0.5, ((0, 16),), jnp.float32)
    couplings = bell_draw(part_keys[5], (FAR, K, K), (FAR_LEAF * K) ** -0.5, 0.375, ((0, 16),), jnp.float32)
    far_owner_keys = jax.random.split(jax.random.fold_in(part_keys[6], 1), FAR // FAR_DEV)
    far_owner_turns = jax.random.permutation(jax.random.fold_in(part_keys[6], 3), FAR // FAR_DEV)
    far_owner = jax.vmap(lambda own, number: shared_out(jax.random.fold_in(part_keys[6], 2), own, number, FAR_DEV, N_LEAF, 1, CAP, 1))(far_owner_keys, far_owner_turns).reshape((FAR, 1))
    far_slot = plant(jax.random.randint(part_keys[7], (FAR,), 0, LEAVES_DEV), jax.random.fold_in(part_keys[7], 1), 0, LEAVES_DEV - 1).astype(jnp.int32)
    leaf_perm = jax.vmap(lambda own: jax.random.permutation(own, M))(jax.random.split(part_keys[8], LEAVES)).reshape((LEAVES, M)).astype(jnp.int32)
    leaf_size = draw_leaf_size(jax.random.fold_in(jax.random.fold_in(seeds[10], part), 71), part)
    return dict(rhs=rhs, near_blocks=near_blocks, near_nbrs=near_nbrs, row_basis=row_basis, col_basis=col_basis, couplings=couplings, far_owner=far_owner, far_slot=far_slot, leaf_perm=leaf_perm, leaf_size=leaf_size)


highest = lax.Precision.HIGHEST

def operator_apply(field, near_blocks, near_nbrs, row_basis, col_basis, couplings, columns, live_mask):
    picked = field[:, near_nbrs]
    near_part = jnp.einsum('rlnm,lnpm->rlp', picked, near_blocks, precision=highest)
    coefficients = jnp.einsum('rlm,lmk->lkr', field, col_basis, precision=highest)
    fetched = coefficients[columns]
    coupled = jnp.einsum('bkj,bjr->bkr', couplings, fetched, precision=highest)
    summed = coupled.reshape(LEAVES, FAR_LEAF, K, R).sum(axis=1)
    far_part = jnp.einsum('lpk,lkr->rlp', row_basis, summed, precision=highest)
    return (near_part + far_part) * live_mask[None]

def inner_product(left_block, right_block):
    return jnp.einsum('rlm,slm->rs', left_block, right_block, precision=highest)

def cholesky_solve_block(gram_matrix, block_vector):
    factor = jnp.linalg.cholesky(gram_matrix)
    solved = jax.scipy.linalg.solve_triangular(factor, block_vector.reshape(R, -1), lower=True)
    return (factor, solved.reshape(block_vector.shape))

def reference(rhs, near_blocks, near_nbrs, row_basis, col_basis, couplings, far_owner, far_slot, leaf_perm, leaf_size):
    positions = jnp.arange(M, dtype=jnp.int32)
    live_mask = (positions[None, :] < leaf_size[:, None]).astype(jnp.float32)
    order = jnp.broadcast_to(leaf_perm[None], rhs.shape).astype(jnp.int32)
    start_block = jnp.take_along_axis(rhs, order, axis=2) * live_mask[None]
    columns = (far_owner[:, 0] * LEAVES_DEV + far_slot).astype(jnp.int32)
    first_factor, first_basis = cholesky_solve_block(inner_product(start_block, start_block), start_block)
    bases_list = [first_basis]
    hessenberg = jnp.zeros(((ITERS + 1) * R, ITERS * R), jnp.float32)
    for j in range(ITERS):
        work_block = operator_apply(bases_list[j], near_blocks, near_nbrs, row_basis, col_basis, couplings, columns, live_mask)
        for i in range(j + 1):
            projected = inner_product(bases_list[i], work_block)
            hessenberg = hessenberg.at[i * R:(i + 1) * R, j * R:(j + 1) * R].set(projected)
            work_block = work_block - jnp.einsum('rs,rlm->slm', projected, bases_list[i], precision=highest)
        new_factor, new_basis = cholesky_solve_block(inner_product(work_block, work_block), work_block)
        hessenberg = hessenberg.at[(j + 1) * R:(j + 2) * R, j * R:(j + 1) * R].set(new_factor.T)
        bases_list.append(new_basis)
    target = jnp.zeros(((ITERS + 1) * R, R), jnp.float32).at[:R].set(first_factor.T)
    normal_matrix = jnp.dot(hessenberg.T, hessenberg, precision=highest)
    small_side = jnp.dot(hessenberg.T, target, precision=highest)
    chol_factor = jnp.linalg.cholesky(normal_matrix)
    weights = jax.scipy.linalg.cho_solve((chol_factor, True), small_side)
    solution = jnp.zeros_like(start_block)
    for j in range(ITERS):
        solution = solution + jnp.einsum('rs,rlm->slm', weights[j * R:(j + 1) * R], bases_list[j], precision=highest)
    return solution
```

```python
import functools

import jax
import jax.numpy as jnp
from jax import lax
from jax.experimental import pallas as pl
from jax.experimental.pallas import tpu as pltpu
from jax.sharding import PartitionSpec as P

F32 = jnp.float32
BF16 = jnp.bfloat16
HIGHEST = lax.Precision.HIGHEST
ITERS = 3
R = 32
M = 128
K = 16
NB = 8
LD = 8
CHUNK = 8
SPAN = 128 // CHUNK
NT = (((1,), (1,)), ((), ()))
NN = (((1,), (0,)), ((), ()))


def split(x):
    hi = x.astype(BF16)
    return hi, (x - hi.astype(F32)).astype(BF16)


def stacked(x):
    hi, lo = split(x)
    return jnp.concatenate([hi, lo], axis=0)


def dot(a, b, dims=NN, precision=None):
    return lax.dot_general(a, b, dims, precision=precision, preferred_element_type=F32)


def dot3(both, hi, lo, dims):
    rows = both.shape[0] // 2
    a = dot(both, hi, dims)
    return a[:rows] + a[rows:] + dot(both[:rows], lo, dims)


def kernel(
    n,
    near_hbm,
    kmat_hbm,
    nbr,
    size,
    rhs,
    perm,
    row_basis,
    col_basis,
    out,
    near_v,
    kmat_v,
    nh,
    nl,
    kh,
    kl,
    ch,
    cl,
    rh,
    rl,
    vs,
    wrecv,
    wsplit,
    crecv,
    gpart,
    grecv,
    gfull,
    mat,
    near_sem,
    kmat_sem,
    wsend,
    wsem,
    csend,
    csem,
    gsend,
    gsem,
    asend,
    asem,
):
    me = lax.axis_index("leaf")
    red = min(n, SPAN)

    loads = [pltpu.make_async_copy(near_hbm.at[l], near_v.at[l], near_sem.at[l]) for l in range(LD)]
    for load in loads:
        load.start()
    kload = pltpu.make_async_copy(kmat_hbm, kmat_v, kmat_sem)
    kload.start()

    barrier = pltpu.get_barrier_semaphore()

    def greet(k, carry):
        pl.semaphore_signal(
            barrier, inc=1, device_id={"leaf": lax.rem(me + k, n)}, device_id_type=pl.DeviceIdType.MESH
        )
        return carry

    lax.fori_loop(1, n, greet, 0)

    row_i = lax.broadcasted_iota(jnp.int32, (M, M), 0)
    col_i = lax.broadcasted_iota(jnp.int32, (M, M), 1)
    live = [
        lax.broadcasted_iota(jnp.int32, (R, M), 1) < size[l] for l in range(LD)
    ]

    for l in range(LD):
        x = rhs[:, l, :]
        hi, rest = split(x)
        rest = x - hi.astype(F32)
        mid, low = split(rest)
        pick = jnp.where((row_i == perm[l : l + 1, :]) & (col_i < size[l]), 1.0, 0.0).astype(BF16)
        parts = dot(jnp.concatenate([hi, mid, low], axis=0), pick)
        vs[l, 0:R, :] = (parts[0:R] + parts[R : 2 * R]) + parts[2 * R :]

    tile_k = lax.broadcasted_iota(jnp.int32, (K, M), 0)
    tile_c = lax.broadcasted_iota(jnp.int32, (K, M), 1)
    for l in range(LD):
        spread = jnp.where(tile_c == tile_k + l * K, 1.0, 0.0)
        hi, lo = split(dot(col_basis[l], spread, NN, HIGHEST))
        ch[l] = hi
        cl[l] = lo
        hi, lo = split(dot(row_basis[l], spread, NN, HIGHEST))
        rh[l] = hi
        rl[l] = lo

    pl.semaphore_wait(barrier, n - 1)

    def halo(step, to_right):
        side = 0 if to_right else 1
        return pltpu.make_async_remote_copy(
            src_ref=vs.at[:, pl.ds(step * R, R), :],
            dst_ref=wrecv.at[step, side],
            send_sem=wsend.at[step, side],
            recv_sem=wsem.at[step, side],
            device_id={"leaf": lax.rem(me + (1 if to_right else n - 1), n)},
            device_id_type=pl.DeviceIdType.MESH,
        )

    def coef(step, rows, target, source):
        return pltpu.make_async_remote_copy(
            src_ref=crecv.at[step, source, pl.ds(0, rows), :],
            dst_ref=crecv.at[step, source, pl.ds(0, rows), :],
            send_sem=csend.at[step, target],
            recv_sem=csem.at[step, source],
            device_id={"leaf": target},
            device_id_type=pl.DeviceIdType.MESH,
        )

    sigma = tau = None
    for step in range(ITERS):
        base = step * R
        rows = R + 8 if step == 0 else R

        @pl.when(me < n - 1)
        def _():
            halo(step, True).start()

        @pl.when(me > 0)
        def _():
            halo(step, False).start()

        coefs = jnp.zeros((R, M), F32)
        for l in range(LD):
            both = stacked(vs[l, base : base + R, :])
            wsplit[LD + l] = both
            coefs = coefs + dot3(both, ch[l], cl[l], NN)
        crecv[step, me, 0:R, :] = coefs

        if step == 0:
            trace = jnp.zeros((M, M), F32)
            power = jnp.zeros((M // 2, M), F32)
            count = jnp.zeros((1, M), F32)
            for l in range(LD):
                loads[l].wait()
                for s in range(NB):
                    x = near_v[l, s]
                    hi, lo = split(x)
                    nh[l, :, s * M : (s + 1) * M] = hi
                    nl[l, :, s * M : (s + 1) * M] = lo
                    power = power + x[: M // 2] * x[: M // 2]
                trace = trace + jnp.where((row_i == col_i) & (row_i < size[l]), near_v[l, 0], 0.0)
                count = count + jnp.where(col_i[:1] < size[l], 1.0, 0.0)
            power = jnp.where(col_i[: M // 2] < M // 2, power, 0.0)
            sums = [jnp.sum(jnp.sum(v, axis=0, keepdims=True), axis=1, keepdims=True) for v in (trace, power, count)]
            tile = lax.broadcasted_iota(jnp.int32, (8, M), 0)
            crecv[step, me, R : R + 8, :] = jnp.where(
                tile == 0, sums[0], jnp.where(tile == 1, sums[1], sums[2])
            )

        def send(k, carry):
            coef(step, rows, lax.rem(me + k, n), me).start()
            return carry

        lax.fori_loop(1, n, send, 0)

        if step == 0:
            kload.wait()
            hi, lo = split(kmat_v[...])
            kh[...] = hi
            kl[...] = lo

        for side in range(2):
            edge = (me > 0) if side == 0 else (me < n - 1)
            first = 0 if side == 0 else 2 * LD

            @pl.when(edge)
            def _():
                halo(step, side == 0).wait_recv()
                for l in range(LD):
                    wsplit[first + l] = stacked(wrecv[step, side, l])

            @pl.when(jnp.logical_not(edge))
            def _():
                for l in range(LD):
                    wsplit[first + l] = jnp.zeros((2 * R, M), BF16)

        near = []
        for l in range(LD):
            both = jnp.concatenate(
                [wsplit[jnp.clip(nbr[l, s] - me * LD + LD, 0, 3 * LD - 1)] for s in range(NB)], axis=1
            )
            near.append(dot3(both, nh[l], nl[l], NT))

        def arrive(k, carry):
            source = lax.rem(me + k, n)
            coef(step, rows, source, source).wait_recv()
            return carry

        lax.fori_loop(1, n, arrive, 0)

        if step == 0:
            total = crecv[0, 0, R : R + 8, :]
            for d in range(1, n):
                total = total + crecv[0, d, R : R + 8, :]
            sigma = total[0:1] / total[2:3]
            tau = jnp.sqrt(jnp.maximum(total[1:2] * (2.0 / (n * LD * (M // 2))), 1.0))

        z = jnp.zeros((R, M), F32)
        for d0 in range(0, n, 16):
            both = jnp.concatenate(
                [stacked(crecv[step, d, 0:R, :]) for d in range(d0, d0 + min(n, 16))], axis=1
            )
            rng = slice(d0 * M, (d0 + min(n, 16)) * M)
            z = z + dot3(both, kh[rng, :], kl[rng, :], NN)
        zz = stacked(z)
        for l in range(LD):
            w = near[l] + dot3(zz, rh[l], rl[l], NT)
            w = jnp.where(live[l], w, 0.0)
            vs[l, base + R : base + 2 * R, :] = (w - sigma * vs[l, base : base + R, :]) / tau

    gram = jnp.zeros((M, M), F32)
    for l in range(LD):
        gram = gram + dot(vs[l], vs[l], NT, HIGHEST)
    for i in range(SPAN):
        gpart[i] = gram[i * CHUNK : (i + 1) * CHUNK]

    def scatter(target, source):
        return pltpu.make_async_remote_copy(
            src_ref=gpart.at[target],
            dst_ref=grecv.at[source],
            send_sem=gsend.at[target],
            recv_sem=gsem.at[source],
            device_id={"leaf": target},
            device_id_type=pl.DeviceIdType.MESH,
        )

    def gather(target, source):
        return pltpu.make_async_remote_copy(
            src_ref=gfull.at[source],
            dst_ref=gfull.at[source],
            send_sem=asend.at[target],
            recv_sem=asem.at[source],
            device_id={"leaf": target},
            device_id_type=pl.DeviceIdType.MESH,
        )

    def when(condition, body):
        if n <= SPAN:
            body()
        else:
            pl.when(condition)(body)

    def over(body, wait):
        def one(k, carry):
            body(lax.rem(me + k, n))
            return carry

        lax.fori_loop(1, n, one, 0)

    over(lambda d: when(d < red, lambda: scatter(d, me).start()), False)

    def reduce():
        over(lambda d: scatter(me, d).wait_recv(), True)
        grecv[me] = gpart[me]
        total = grecv[0]
        for d in range(1, n):
            total = total + grecv[d]
        gfull[me] = total
        over(lambda d: gather(d, me).start(), False)

    when(me < red, reduce)
    over(lambda d: when(d < red, lambda: gather(me, d).wait_recv()), True)

    full = gfull[...].reshape(M, M)
    u = tau * full[R:] + sigma * full[: M - R]
    turned = pltpu.roll(u, M - R, axis=1)
    lane = lax.broadcasted_iota(jnp.int32, (M - R, M), 1)
    sub = lax.broadcasted_iota(jnp.int32, (M - R, M), 0)
    a = jnp.where(lane < M - R, tau * turned + sigma * u, turned)
    mat[0 : M - R, :] = a

    def eliminate(i, carry):
        a = mat[0 : M - R, :]
        line = mat[pl.ds(i, 1), :]
        column = jnp.sum(jnp.where(lane == i, a, 0.0), axis=1, keepdims=True)
        pivot = jnp.sum(jnp.where(lane[:1] == i, line, 0.0), axis=1, keepdims=True)
        line = line / pivot
        mat[0 : M - R, :] = jnp.where(sub == i, line, a - column * line)
        return carry

    lax.fori_loop(0, M - R, eliminate, 0)
    mat[M - R :, :] = jnp.zeros((R, M), F32)
    weights = mat[...].T[M - R :, :]
    for l in range(LD):
        out[:, l, :] = dot(weights, vs[l], NN, HIGHEST)

    for step in range(ITERS):

        @pl.when(me < n - 1)
        def _():
            halo(step, True).wait_send()

        @pl.when(me > 0)
        def _():
            halo(step, False).wait_send()

        rows = R + 8 if step == 0 else R
        over(lambda d: coef(step, rows, d, me).wait_send(), True)
    over(lambda d: when(d < red, lambda: scatter(d, me).wait_send()), True)
    when(me < red, lambda: over(lambda d: gather(d, me).wait_send(), True))


def shards(
    rhs,
    near_blocks,
    near_nbrs,
    row_basis,
    col_basis,
    couplings,
    far_owner,
    far_slot,
    leaf_perm,
    leaf_size,
):
    n = lax.axis_size("leaf")
    columns = (far_owner[:, 0] * LD + far_slot).reshape(LD, -1)
    far_leaf = columns.shape[1]
    chosen = (columns[:, :, None] == jnp.arange(n * LD, dtype=jnp.int32)).astype(F32)
    kmat = jnp.einsum(
        "lbj,lbkq->jqlk", chosen, couplings.reshape(LD, far_leaf, K, K), precision=HIGHEST
    ).reshape(n * M, M)
    vmem = pl.BlockSpec(memory_space=pltpu.VMEM)
    smem = pl.BlockSpec(memory_space=pltpu.SMEM)
    anyspace = pl.BlockSpec(memory_space=pl.ANY)
    dma = pltpu.SemaphoreType.DMA
    return pl.pallas_call(
        functools.partial(kernel, n),
        out_shape=jax.ShapeDtypeStruct((R, LD, M), F32),
        in_specs=[anyspace, anyspace, smem, smem, vmem, vmem, vmem, vmem],
        out_specs=vmem,
        scratch_shapes=[
            pltpu.VMEM((LD, NB, M, M), F32),
            pltpu.VMEM((n * M, M), F32),
            pltpu.VMEM((LD, M, NB * M), BF16),
            pltpu.VMEM((LD, M, NB * M), BF16),
            pltpu.VMEM((n * M, M), BF16),
            pltpu.VMEM((n * M, M), BF16),
            pltpu.VMEM((LD, M, M), BF16),
            pltpu.VMEM((LD, M, M), BF16),
            pltpu.VMEM((LD, M, M), BF16),
            pltpu.VMEM((LD, M, M), BF16),
            pltpu.VMEM((LD, M, M), F32),
            pltpu.VMEM((ITERS, 2, LD, R, M), F32),
            pltpu.VMEM((3 * LD, 2 * R, M), BF16),
            pltpu.VMEM((ITERS, n, R + 8, M), F32),
            pltpu.VMEM((SPAN, CHUNK, M), F32),
            pltpu.VMEM((n, CHUNK, M), F32),
            pltpu.VMEM((SPAN, CHUNK, M), F32),
            pltpu.VMEM((M, M), F32),
            dma((LD,)),
            dma,
            dma((ITERS, 2)),
            dma((ITERS, 2)),
            dma((ITERS, n)),
            dma((ITERS, n)),
            dma((n,)),
            dma((n,)),
            dma((n,)),
            dma((n,)),
        ],
        compiler_params=pltpu.CompilerParams(
            collective_id=0, has_side_effects=True, vmem_limit_bytes=48 * 1024 * 1024
        ),
    )(near_blocks, kmat, near_nbrs, leaf_size, rhs, leaf_perm, row_basis, col_basis)


def solution(mesh):
    in_specs = (
        P(None, ("grp", "leaf"), None),
        P(("grp", "leaf"), None, None, None),
        P(("grp", "leaf"), None),
        P(("grp", "leaf"), None, None),
        P(("grp", "leaf"), None, None),
        P(("grp", "leaf"), None, None),
        P(("grp", "leaf"), None),
        P(("grp", "leaf")),
        P(("grp", "leaf"), None),
        P(("grp", "leaf")),
    )
    out_specs = P(None, ("grp", "leaf"), None)
    return jax.shard_map(shards, mesh=mesh, in_specs=in_specs, out_specs=out_specs, check_vma=False)
```

```python
import functools

import jax
import jax.numpy as jnp
from jax import lax
from jax.experimental import pallas as pl
from jax.experimental.pallas import tpu as pltpu
from jax.sharding import PartitionSpec as P

F32 = jnp.float32
BF16 = jnp.bfloat16
HIGHEST = lax.Precision.HIGHEST
ITERS = 3
R = 32
M = 128
K = 16
NB = 8
LD = 8
CHUNK = 8
PRE = 96
SPAN = PRE // CHUNK
NT = (((1,), (1,)), ((), ()))
NN = (((1,), (0,)), ((), ()))


def split(x):
    hi = x.astype(BF16)
    return hi, (x - hi.astype(F32)).astype(BF16)


def stacked(x):
    hi, lo = split(x)
    return jnp.concatenate([hi, lo], axis=0)


def dot(a, b, dims=NN, precision=None):
    return lax.dot_general(a, b, dims, precision=precision, preferred_element_type=F32)


def dot3(both, hi, lo, dims):
    rows = both.shape[0] // 2
    a = dot(both, hi, dims)
    return a[:rows] + a[rows:] + dot(both[:rows], lo, dims)


def kernel(
    n,
    near_hbm,
    nbr_hbm,
    size_hbm,
    rhs_hbm,
    perm_hbm,
    row_hbm,
    col_hbm,
    cpl_hbm,
    owner_hbm,
    slot_hbm,
    out,
    nbr,
    size,
    rhs,
    perm,
    row_basis,
    col_basis,
    cpl,
    owner,
    slot,
    near_v,
    nh,
    nl,
    kh,
    kl,
    ch,
    cl,
    rh,
    rl,
    vs,
    wrecv,
    wsplit,
    crecv,
    gpart,
    grecv,
    gfull,
    lrecv,
    mat,
    small_sem,
    near_sem,
    wsend,
    wsem,
    csend,
    csem,
    gsend,
    gsem,
    asend,
    asem,
    lsend,
    lsem,
):
    me = lax.axis_index("leaf")
    red = PRE // CHUNK

    pairs = (
        (size_hbm, size),
        (rhs_hbm, rhs),
        (perm_hbm, perm),
        (col_hbm, col_basis),
        (row_hbm, row_basis),
        (nbr_hbm, nbr),
        (cpl_hbm, cpl),
        (owner_hbm, owner),
        (slot_hbm, slot),
    )
    smalls = [pltpu.make_async_copy(a, b, small_sem.at[i]) for i, (a, b) in enumerate(pairs)]
    for load in smalls:
        load.start()
    loads = [pltpu.make_async_copy(near_hbm.at[l], near_v.at[l], near_sem.at[l]) for l in range(LD)]
    for load in loads:
        load.start()

    barrier = pltpu.get_barrier_semaphore()

    def greet(k, carry):
        pl.semaphore_signal(
            barrier, inc=1, device_id={"leaf": lax.rem(me + k, n)}, device_id_type=pl.DeviceIdType.MESH
        )
        return carry

    lax.fori_loop(1, n, greet, 0)

    for load in smalls:
        load.wait()

    row_i = lax.broadcasted_iota(jnp.int32, (M, M), 0)
    col_i = lax.broadcasted_iota(jnp.int32, (M, M), 1)
    live = [
        lax.broadcasted_iota(jnp.int32, (R, M), 1) < size[l] for l in range(LD)
    ]

    for l in range(LD):
        x = rhs[:, l, :]
        hi, rest = split(x)
        rest = x - hi.astype(F32)
        mid, low = split(rest)
        pick = jnp.where((row_i == perm[l : l + 1, :]) & (col_i < size[l]), 1.0, 0.0).astype(BF16)
        parts = dot(jnp.concatenate([hi, mid, low], axis=0), pick)
        vs[l, 0:R, :] = (parts[0:R] + parts[R : 2 * R]) + parts[2 * R :]

    group = lax.broadcasted_iota(jnp.int32, (K, LD, M), 1)
    for l in range(LD):
        wide = jnp.broadcast_to(col_basis[l][:, None, :], (K, LD, M))
        hi, lo = split(jnp.where(group == l, wide, 0.0).reshape(M, M))
        ch[l] = hi
        cl[l] = lo
        tall = jnp.concatenate([row_basis[l]] * LD, axis=0)
        hi, lo = split(jnp.where(row_i // K == l, tall, 0.0))
        rh[l] = hi
        rl[l] = lo

    pl.semaphore_wait(barrier, n - 1)

    def halo(step, to_right):
        side = 0 if to_right else 1
        return pltpu.make_async_remote_copy(
            src_ref=vs.at[:, pl.ds(step * R, R), :],
            dst_ref=wrecv.at[step, side],
            send_sem=wsend.at[step, side],
            recv_sem=wsem.at[step, side],
            device_id={"leaf": lax.rem(me + (1 if to_right else n - 1), n)},
            device_id_type=pl.DeviceIdType.MESH,
        )

    def coef(step, rows, target, source):
        return pltpu.make_async_remote_copy(
            src_ref=crecv.at[step, source, pl.ds(0, rows), :],
            dst_ref=crecv.at[step, source, pl.ds(0, rows), :],
            send_sem=csend.at[step, target],
            recv_sem=csem.at[step, source],
            device_id={"leaf": target},
            device_id_type=pl.DeviceIdType.MESH,
        )

    def scatter(target, source):
        return pltpu.make_async_remote_copy(
            src_ref=gpart.at[target],
            dst_ref=grecv.at[source],
            send_sem=gsend.at[target],
            recv_sem=gsem.at[source],
            device_id={"leaf": target},
            device_id_type=pl.DeviceIdType.MESH,
        )

    def gather(target, source):
        return pltpu.make_async_remote_copy(
            src_ref=gfull.at[source],
            dst_ref=gfull.at[source],
            send_sem=asend.at[target],
            recv_sem=asem.at[source],
            device_id={"leaf": target},
            device_id_type=pl.DeviceIdType.MESH,
        )

    def final(target, source):
        return pltpu.make_async_remote_copy(
            src_ref=lrecv.at[source],
            dst_ref=lrecv.at[source],
            send_sem=lsend.at[target],
            recv_sem=lsem.at[source],
            device_id={"leaf": target},
            device_id_type=pl.DeviceIdType.MESH,
        )

    def when(condition, body):
        pl.when(condition)(body)

    def over(body):
        def one(k, carry):
            body(lax.rem(me + k, n))
            return carry

        lax.fori_loop(1, n, one, 0)

    def reduce():
        over(lambda d: scatter(me, d).wait_recv())
        grecv[me] = gpart[me]
        total = grecv[0]
        for d in range(1, n):
            total = total + grecv[d]
        gfull[me] = total
        over(lambda d: gather(d, me).start())

    sigma = tau = None
    for step in range(ITERS):
        base = step * R
        rows = R + 8 if step == 0 else R

        @pl.when(me < n - 1)
        def _():
            halo(step, True).start()

        @pl.when(me > 0)
        def _():
            halo(step, False).start()

        coefs = jnp.zeros((R, M), F32)
        for l in range(LD):
            both = stacked(vs[l, base : base + R, :])
            wsplit[LD + l] = both
            coefs = coefs + dot3(both, ch[l], cl[l], NT)
        crecv[step, me, 0:R, :] = coefs

        if step == 0:
            trace = jnp.zeros((M, M), F32)
            power = jnp.zeros((M // 2, M), F32)
            count = jnp.zeros((1, M), F32)
            for l in range(LD):
                loads[l].wait()
                for s in range(NB):
                    x = near_v[l, s]
                    hi, lo = split(x)
                    nh[l, :, s * M : (s + 1) * M] = hi
                    nl[l, :, s * M : (s + 1) * M] = lo
                    power = power + x[: M // 2] * x[: M // 2]
                trace = trace + jnp.where((row_i == col_i) & (row_i < size[l]), near_v[l, 0], 0.0)
                count = count + jnp.where(col_i[:1] < size[l], 1.0, 0.0)
            power = jnp.where(col_i[: M // 2] < M // 2, power, 0.0)
            sums = [jnp.sum(jnp.sum(v, axis=0, keepdims=True), axis=1, keepdims=True) for v in (trace, power, count)]
            tile = lax.broadcasted_iota(jnp.int32, (8, M), 0)
            crecv[step, me, R : R + 8, :] = jnp.where(
                tile == 0, sums[0], jnp.where(tile == 1, sums[1], sums[2])
            )

        def send(k, carry):
            coef(step, rows, lax.rem(me + k, n), me).start()
            return carry

        lax.fori_loop(1, n, send, 0)

        if step == 0:
            columns = owner[...] * LD + slot[...]
            chosen = jnp.where(
                lax.broadcasted_iota(jnp.int32, (n * LD, M), 0) == columns, 1.0, 0.0
            ).astype(BF16)
            far_leaf = M // LD
            for k in range(0, K, 2):
                both = []
                for k2 in (k, k + 1):
                    tall = jnp.concatenate([cpl[:, k2, :]] * LD, axis=0)
                    hi, lo = split(jnp.where(row_i // K == col_i // far_leaf, tall, 0.0))
                    both.append((dot(chosen, hi, NT) + dot(chosen, lo, NT)).reshape(n, LD, M))
                hi, lo = split(jnp.concatenate(both, axis=1))
                kh[:, k * LD : (k + 2) * LD, :] = hi
                kl[:, k * LD : (k + 2) * LD, :] = lo

        if step == ITERS - 1:
            early = jnp.zeros((PRE, PRE), F32)
            for l in range(LD):
                early = early + dot(vs[l, 0:PRE, :], vs[l, 0:PRE, :], NT, HIGHEST)
            early = jnp.concatenate([early, jnp.zeros((PRE, M - PRE), F32)], axis=1)
            for i in range(SPAN):
                gpart[i] = early[i * CHUNK : (i + 1) * CHUNK]
            over(lambda d: when(d < red, lambda: scatter(d, me).start()))

        for side in range(2):
            edge = (me > 0) if side == 0 else (me < n - 1)
            first = 0 if side == 0 else 2 * LD

            @pl.when(edge)
            def _():
                halo(step, side == 0).wait_recv()
                for l in range(LD):
                    wsplit[first + l] = stacked(wrecv[step, side, l])

            @pl.when(jnp.logical_not(edge))
            def _():
                for l in range(LD):
                    wsplit[first + l] = jnp.zeros((2 * R, M), BF16)

        near = []
        for l in range(LD):
            both = jnp.concatenate(
                [wsplit[jnp.clip(nbr[l, s] - me * LD + LD, 0, 3 * LD - 1)] for s in range(NB)], axis=1
            )
            near.append(dot3(both, nh[l], nl[l], NT))

        if step == ITERS - 1:
            when(me < red, reduce)

        def arrive(k, carry):
            source = lax.rem(me + k, n)
            coef(step, rows, source, source).wait_recv()
            return carry

        lax.fori_loop(1, n, arrive, 0)

        if step == 0:
            total = crecv[0, 0, R : R + 8, :]
            for d in range(1, n):
                total = total + crecv[0, d, R : R + 8, :]
            sigma = total[0:1] / total[2:3]
            tau = jnp.sqrt(jnp.maximum(total[1:2] * (2.0 / (n * LD * (M // 2))), 1.0))

        z = jnp.zeros((R, M), F32)
        for d0 in range(0, n, 16):
            both = jnp.concatenate(
                [stacked(crecv[step, d, 0:R, :]) for d in range(d0, d0 + min(n, 16))], axis=1
            )
            rng = slice(d0, d0 + min(n, 16))
            z = z + dot3(both, kh[rng].reshape(-1, M), kl[rng].reshape(-1, M), NN)
        zz = stacked(z)
        for l in range(LD):
            w = near[l] + dot3(zz, rh[l], rl[l], NN)
            w = jnp.where(live[l], w, 0.0)
            vs[l, base + R : base + 2 * R, :] = (w - sigma * vs[l, base : base + R, :]) / tau

    last = jnp.zeros((R, M), F32)
    for l in range(LD):
        last = last + dot(vs[l, PRE:, :], vs[l], NT, HIGHEST)
    lrecv[me] = last
    over(lambda d: final(d, me).start())
    over(lambda d: when(d < red, lambda: gather(me, d).wait_recv()))
    over(lambda d: final(d, d).wait_recv())
    last = lrecv[0]
    for d in range(1, n):
        last = last + lrecv[d]
    first = gfull[...].reshape(PRE, M)
    turned = jnp.concatenate([jnp.zeros((PRE, M), F32), last], axis=0).T
    lane = lax.broadcasted_iota(jnp.int32, (PRE, M), 1)
    sub = lax.broadcasted_iota(jnp.int32, (PRE, M), 0)
    full = jnp.concatenate([jnp.where(lane < PRE, first, turned[:PRE]), last], axis=0)
    u = tau * full[R:] + sigma * full[: M - R]
    turned = pltpu.roll(u, M - R, axis=1)
    a = jnp.where(lane < M - R, tau * turned + sigma * u, turned)
    for i in range(PRE):
        line = a[i : i + 1, :]
        line = line * (1.0 / line[:, i : i + 1])
        a = jnp.where(sub == i, line, a - a[:, i : i + 1] * line)
    mat[0:PRE, :] = a
    mat[M - R :, :] = jnp.zeros((R, M), F32)
    weights = mat[...].T[M - R :, :]
    for l in range(LD):
        out[:, l, :] = dot(weights, vs[l], NN, HIGHEST)

    for step in range(ITERS):

        @pl.when(me < n - 1)
        def _():
            halo(step, True).wait_send()

        @pl.when(me > 0)
        def _():
            halo(step, False).wait_send()

        rows = R + 8 if step == 0 else R
        over(lambda d: coef(step, rows, d, me).wait_send())
    over(lambda d: when(d < red, lambda: scatter(d, me).wait_send()))
    when(me < red, lambda: over(lambda d: gather(d, me).wait_send()))
    over(lambda d: final(d, me).wait_send())


def shards(
    rhs,
    near_blocks,
    near_nbrs,
    row_basis,
    col_basis,
    couplings,
    far_owner,
    far_slot,
    leaf_perm,
    leaf_size,
):
    n = lax.axis_size("leaf")
    vmem = pl.BlockSpec(memory_space=pltpu.VMEM)
    anyspace = pl.BlockSpec(memory_space=pltpu.HBM)
    dma = pltpu.SemaphoreType.DMA
    return pl.pallas_call(
        functools.partial(kernel, n),
        out_shape=jax.ShapeDtypeStruct((R, LD, M), F32),
        in_specs=[anyspace] * 10,
        out_specs=vmem,
        scratch_shapes=[
            pltpu.SMEM((LD, NB), jnp.int32),
            pltpu.SMEM((LD,), jnp.int32),
            pltpu.VMEM((R, LD, M), F32),
            pltpu.VMEM((LD, M), jnp.int32),
            pltpu.VMEM((LD, K, M), F32),
            pltpu.VMEM((LD, K, M), F32),
            pltpu.VMEM((K, K, M), F32),
            pltpu.VMEM((1, M), jnp.int32),
            pltpu.VMEM((1, M), jnp.int32),
            pltpu.VMEM((LD, NB, M, M), F32),
            pltpu.VMEM((LD, M, NB * M), BF16),
            pltpu.VMEM((LD, M, NB * M), BF16),
            pltpu.VMEM((n, M, M), BF16),
            pltpu.VMEM((n, M, M), BF16),
            pltpu.VMEM((LD, M, M), BF16),
            pltpu.VMEM((LD, M, M), BF16),
            pltpu.VMEM((LD, M, M), BF16),
            pltpu.VMEM((LD, M, M), BF16),
            pltpu.VMEM((LD, M, M), F32),
            pltpu.VMEM((ITERS, 2, LD, R, M), F32),
            pltpu.VMEM((3 * LD, 2 * R, M), BF16),
            pltpu.VMEM((ITERS, n, R + 8, M), F32),
            pltpu.VMEM((SPAN, CHUNK, M), F32),
            pltpu.VMEM((n, CHUNK, M), F32),
            pltpu.VMEM((SPAN, CHUNK, M), F32),
            pltpu.VMEM((n, R, M), F32),
            pltpu.VMEM((M, M), F32),
            dma((9,)),
            dma((LD,)),
            dma((ITERS, 2)),
            dma((ITERS, 2)),
            dma((ITERS, n)),
            dma((ITERS, n)),
            dma((n,)),
            dma((n,)),
            dma((n,)),
            dma((n,)),
            dma((n,)),
            dma((n,)),
        ],
        compiler_params=pltpu.CompilerParams(
            collective_id=0, has_side_effects=True, vmem_limit_bytes=56 * 1024 * 1024
        ),
    )(
        near_blocks,
        near_nbrs,
        leaf_size,
        rhs,
        leaf_perm,
        jnp.swapaxes(row_basis, 1, 2),
        jnp.swapaxes(col_basis, 1, 2),
        jnp.transpose(couplings, (1, 2, 0)),
        far_owner.reshape(1, -1),
        far_slot.reshape(1, -1),
    )


def solution(mesh):
    in_specs = (
        P(None, ("grp", "leaf"), None),
        P(("grp", "leaf"), None, None, None),
        P(("grp", "leaf"), None),
        P(("grp", "leaf"), None, None),
        P(("grp", "leaf"), None, None),
        P(("grp", "leaf"), None, None),
        P(("grp", "leaf"), None),
        P(("grp", "leaf")),
        P(("grp", "leaf"), None),
        P(("grp", "leaf")),
    )
    out_specs = P(None, ("grp", "leaf"), None)
    return jax.shard_map(shards, mesh=mesh, in_specs=in_specs, out_specs=out_specs, check_vma=False)
```

```python
import functools

import jax
import jax.numpy as jnp
from jax import lax
from jax.experimental import pallas as pl
from jax.experimental.pallas import tpu as pltpu
from jax.sharding import PartitionSpec as P

F32 = jnp.float32
BF16 = jnp.bfloat16
HIGHEST = lax.Precision.HIGHEST
ITERS = 3
R = 32
M = 128
K = 16
NB = 8
LD = 8
CHUNK = 8
PRE = 96
SPAN = PRE // CHUNK
NT = (((1,), (1,)), ((), ()))
NN = (((1,), (0,)), ((), ()))


def split(x):
    hi = x.astype(BF16)
    return hi, (x - hi.astype(F32)).astype(BF16)


def stacked(x):
    hi, lo = split(x)
    return jnp.concatenate([hi, lo], axis=0)


def dot(a, b, dims=NN, precision=None):
    return lax.dot_general(a, b, dims, precision=precision, preferred_element_type=F32)


def dot3(both, hi, lo, dims):
    rows = both.shape[0] // 2
    a = dot(both, hi, dims)
    return a[:rows] + a[rows:] + dot(both[:rows], lo, dims)


def kernel(
    n,
    near_hbm,
    nbr_hbm,
    size_hbm,
    rhs_hbm,
    perm_hbm,
    row_hbm,
    col_hbm,
    cpl_hbm,
    owner_hbm,
    slot_hbm,
    out,
    nbr,
    size,
    rhs,
    perm,
    row_basis,
    col_basis,
    cpl,
    owner,
    slot,
    near_v,
    nh,
    nl,
    kh,
    kl,
    ch,
    cl,
    rh,
    rl,
    vs,
    wrecv,
    wsplit,
    crecv,
    gpart,
    grecv,
    gfull,
    lrecv,
    mat,
    small_sem,
    near_sem,
    wsend,
    wsem,
    csend,
    csem,
    fsend,
    gsend,
    gsem,
    asend,
    asem,
    lsend,
    lsem,
):
    me = lax.axis_index("leaf")
    red = PRE // CHUNK

    pairs = (
        (size_hbm, size),
        (rhs_hbm, rhs),
        (perm_hbm, perm),
        (col_hbm, col_basis),
        (row_hbm, row_basis),
        (nbr_hbm, nbr),
        (cpl_hbm, cpl),
        (owner_hbm, owner),
        (slot_hbm, slot),
    )
    smalls = [pltpu.make_async_copy(a, b, small_sem.at[i]) for i, (a, b) in enumerate(pairs)]
    for load in smalls:
        load.start()
    loads = [pltpu.make_async_copy(near_hbm.at[l], near_v.at[l], near_sem.at[l]) for l in range(LD)]
    for load in loads:
        load.start()

    barrier = pltpu.get_barrier_semaphore()

    def greet(k, carry):
        pl.semaphore_signal(
            barrier, inc=1, device_id={"leaf": lax.rem(me + k, n)}, device_id_type=pl.DeviceIdType.MESH
        )
        return carry

    lax.fori_loop(1, n, greet, 0)

    for load in smalls:
        load.wait()

    row_i = lax.broadcasted_iota(jnp.int32, (M, M), 0)
    col_i = lax.broadcasted_iota(jnp.int32, (M, M), 1)
    live = [
        lax.broadcasted_iota(jnp.int32, (R, M), 1) < size[l] for l in range(LD)
    ]

    for l in range(LD):
        x = rhs[:, l, :]
        hi, rest = split(x)
        rest = x - hi.astype(F32)
        mid, low = split(rest)
        pick = jnp.where((row_i == perm[l : l + 1, :]) & (col_i < size[l]), 1.0, 0.0).astype(BF16)
        parts = dot(jnp.concatenate([hi, mid, low], axis=0), pick)
        vs[l, 0:R, :] = (parts[0:R] + parts[R : 2 * R]) + parts[2 * R :]

    group = lax.broadcasted_iota(jnp.int32, (K, LD, M), 1)
    for l in range(LD):
        wide = jnp.broadcast_to(col_basis[l][:, None, :], (K, LD, M))
        hi, lo = split(jnp.where(group == l, wide, 0.0).reshape(M, M))
        ch[l] = hi
        cl[l] = lo
        tall = jnp.concatenate([row_basis[l]] * LD, axis=0)
        hi, lo = split(jnp.where(row_i // K == l, tall, 0.0))
        rh[l] = hi
        rl[l] = lo

    pl.semaphore_wait(barrier, n - 1)

    def halo(step, to_right):
        side = 0 if to_right else 1
        return pltpu.make_async_remote_copy(
            src_ref=vs.at[:, pl.ds(step * R, R), :],
            dst_ref=wrecv.at[step, side],
            send_sem=wsend.at[step, side],
            recv_sem=wsem.at[step, side],
            device_id={"leaf": lax.rem(me + (1 if to_right else n - 1), n)},
            device_id_type=pl.DeviceIdType.MESH,
        )

    def coef(step, rows, target, source):
        return pltpu.make_async_remote_copy(
            src_ref=crecv.at[step, source, pl.ds(0, rows), :],
            dst_ref=crecv.at[step, source, pl.ds(0, rows), :],
            send_sem=csend.at[step, target],
            recv_sem=csem.at[step, source],
            device_id={"leaf": target},
            device_id_type=pl.DeviceIdType.MESH,
        )

    partner = me + 1 - 2 * lax.rem(me, 2)

    def relay(step, rows, source):
        return pltpu.make_async_remote_copy(
            src_ref=crecv.at[step, source, pl.ds(0, rows), :],
            dst_ref=crecv.at[step, source, pl.ds(0, rows), :],
            send_sem=fsend.at[step, source],
            recv_sem=csem.at[step, source],
            device_id={"leaf": partner},
            device_id_type=pl.DeviceIdType.MESH,
        )

    def scatter(target, source):
        return pltpu.make_async_remote_copy(
            src_ref=gpart.at[target],
            dst_ref=grecv.at[source],
            send_sem=gsend.at[target],
            recv_sem=gsem.at[source],
            device_id={"leaf": target},
            device_id_type=pl.DeviceIdType.MESH,
        )

    def gather(target, source):
        return pltpu.make_async_remote_copy(
            src_ref=gfull.at[source],
            dst_ref=gfull.at[source],
            send_sem=asend.at[target],
            recv_sem=asem.at[source],
            device_id={"leaf": target},
            device_id_type=pl.DeviceIdType.MESH,
        )

    def final(target, source):
        return pltpu.make_async_remote_copy(
            src_ref=lrecv.at[source],
            dst_ref=lrecv.at[source],
            send_sem=lsend.at[target],
            recv_sem=lsem.at[source],
            device_id={"leaf": target},
            device_id_type=pl.DeviceIdType.MESH,
        )

    def when(condition, body):
        pl.when(condition)(body)

    def over(body):
        def one(k, carry):
            body(lax.rem(me + k, n))
            return carry

        lax.fori_loop(1, n, one, 0)

    def reduce():
        over(lambda d: scatter(me, d).wait_recv())
        grecv[me] = gpart[me]
        total = grecv[0]
        for d in range(1, n):
            total = total + grecv[d]
        gfull[me] = total
        over(lambda d: gather(d, me).start())

    sigma = tau = None
    for step in range(ITERS):
        base = step * R
        rows = R + 8 if step == 0 else R

        @pl.when(me < n - 1)
        def _():
            halo(step, True).start()

        @pl.when(me > 0)
        def _():
            halo(step, False).start()

        coefs = jnp.zeros((R, M), F32)
        for l in range(LD):
            both = stacked(vs[l, base : base + R, :])
            wsplit[LD + l] = both
            coefs = coefs + dot3(both, ch[l], cl[l], NT)
        crecv[step, me, 0:R, :] = coefs

        if step == 0:
            trace = jnp.zeros((M, M), F32)
            power = jnp.zeros((M // 2, M), F32)
            count = jnp.zeros((1, M), F32)
            for l in range(LD):
                loads[l].wait()
                for s in range(NB):
                    x = near_v[l, s]
                    hi, lo = split(x)
                    nh[l, :, s * M : (s + 1) * M] = hi
                    nl[l, :, s * M : (s + 1) * M] = lo
                    power = power + x[: M // 2] * x[: M // 2]
                trace = trace + jnp.where((row_i == col_i) & (row_i < size[l]), near_v[l, 0], 0.0)
                count = count + jnp.where(col_i[:1] < size[l], 1.0, 0.0)
            power = jnp.where(col_i[: M // 2] < M // 2, power, 0.0)
            sums = [jnp.sum(jnp.sum(v, axis=0, keepdims=True), axis=1, keepdims=True) for v in (trace, power, count)]
            tile = lax.broadcasted_iota(jnp.int32, (8, M), 0)
            crecv[step, me, R : R + 8, :] = jnp.where(
                tile == 0, sums[0], jnp.where(tile == 1, sums[1], sums[2])
            )

        coef(step, rows, partner, me).start()

        def send(k, carry):
            coef(step, rows, lax.rem(me + 2 * k, n), me).start()
            return carry

        lax.fori_loop(1, n // 2, send, 0)

        if step == 0:
            columns = owner[...] * LD + slot[...]
            chosen = jnp.where(
                lax.broadcasted_iota(jnp.int32, (n * LD, M), 0) == columns, 1.0, 0.0
            ).astype(BF16)
            far_leaf = M // LD
            for k in range(0, K, 2):
                both = []
                for k2 in (k, k + 1):
                    tall = jnp.concatenate([cpl[:, k2, :]] * LD, axis=0)
                    hi, lo = split(jnp.where(row_i // K == col_i // far_leaf, tall, 0.0))
                    both.append((dot(chosen, hi, NT) + dot(chosen, lo, NT)).reshape(n, LD, M))
                hi, lo = split(jnp.concatenate(both, axis=1))
                kh[:, k * LD : (k + 2) * LD, :] = hi
                kl[:, k * LD : (k + 2) * LD, :] = lo

        if step == ITERS - 1:
            early = jnp.zeros((PRE, PRE), F32)
            for l in range(LD):
                early = early + dot(vs[l, 0:PRE, :], vs[l, 0:PRE, :], NT, HIGHEST)
            early = jnp.concatenate([early, jnp.zeros((PRE, M - PRE), F32)], axis=1)
            for i in range(SPAN):
                gpart[i] = early[i * CHUNK : (i + 1) * CHUNK]
            over(lambda d: when(d < red, lambda: scatter(d, me).start()))

        for side in range(2):
            edge = (me > 0) if side == 0 else (me < n - 1)
            first = 0 if side == 0 else 2 * LD

            @pl.when(edge)
            def _():
                halo(step, side == 0).wait_recv()
                for l in range(LD):
                    wsplit[first + l] = stacked(wrecv[step, side, l])

            @pl.when(jnp.logical_not(edge))
            def _():
                for l in range(LD):
                    wsplit[first + l] = jnp.zeros((2 * R, M), BF16)

        def forward(k, carry):
            source = lax.rem(me + 2 * k, n)
            coef(step, rows, source, source).wait_recv()
            relay(step, rows, source).start()
            return carry

        lax.fori_loop(1, n // 2, forward, 0)

        near = []
        for l in range(LD):
            both = jnp.concatenate(
                [wsplit[jnp.clip(nbr[l, s] - me * LD + LD, 0, 3 * LD - 1)] for s in range(NB)], axis=1
            )
            near.append(dot3(both, nh[l], nl[l], NT))

        if step == ITERS - 1:
            when(me < red, reduce)

        def arrive(k, carry):
            source = lax.rem(partner + 2 * k, n)
            coef(step, rows, source, source).wait_recv()
            return carry

        lax.fori_loop(0, n // 2, arrive, 0)

        if step == 0:
            total = crecv[0, 0, R : R + 8, :]
            for d in range(1, n):
                total = total + crecv[0, d, R : R + 8, :]
            sigma = total[0:1] / total[2:3]
            tau = jnp.sqrt(jnp.maximum(total[1:2] * (2.0 / (n * LD * (M // 2))), 1.0))

        z = jnp.zeros((R, M), F32)
        for d0 in range(0, n, 16):
            both = jnp.concatenate(
                [stacked(crecv[step, d, 0:R, :]) for d in range(d0, d0 + min(n, 16))], axis=1
            )
            rng = slice(d0, d0 + min(n, 16))
            z = z + dot3(both, kh[rng].reshape(-1, M), kl[rng].reshape(-1, M), NN)
        zz = stacked(z)
        for l in range(LD):
            w = near[l] + dot3(zz, rh[l], rl[l], NN)
            w = jnp.where(live[l], w, 0.0)
            vs[l, base + R : base + 2 * R, :] = (w - sigma * vs[l, base : base + R, :]) / tau

    last = jnp.zeros((R, M), F32)
    for l in range(LD):
        last = last + dot(vs[l, PRE:, :], vs[l], NT, HIGHEST)
    lrecv[me] = last
    over(lambda d: final(d, me).start())
    over(lambda d: when(d < red, lambda: gather(me, d).wait_recv()))
    over(lambda d: final(d, d).wait_recv())
    last = lrecv[0]
    for d in range(1, n):
        last = last + lrecv[d]
    first = gfull[...].reshape(PRE, M)
    turned = jnp.concatenate([jnp.zeros((PRE, M), F32), last], axis=0).T
    lane = lax.broadcasted_iota(jnp.int32, (PRE, M), 1)
    sub = lax.broadcasted_iota(jnp.int32, (PRE, M), 0)
    full = jnp.concatenate([jnp.where(lane < PRE, first, turned[:PRE]), last], axis=0)
    u = tau * full[R:] + sigma * full[: M - R]
    turned = pltpu.roll(u, M - R, axis=1)
    a = jnp.where(lane < M - R, tau * turned + sigma * u, turned)
    for i in range(PRE):
        line = a[i : i + 1, :]
        line = line * (1.0 / line[:, i : i + 1])
        a = jnp.where(sub == i, line, a - a[:, i : i + 1] * line)
    mat[0:PRE, :] = a
    mat[M - R :, :] = jnp.zeros((R, M), F32)
    weights = mat[...].T[M - R :, :]
    for l in range(LD):
        out[:, l, :] = dot(weights, vs[l], NN, HIGHEST)

    for step in range(ITERS):

        @pl.when(me < n - 1)
        def _():
            halo(step, True).wait_send()

        @pl.when(me > 0)
        def _():
            halo(step, False).wait_send()

        rows = R + 8 if step == 0 else R
        coef(step, rows, partner, me).wait_send()

        def sent(k, carry):
            other = lax.rem(me + 2 * k, n)
            coef(step, rows, other, me).wait_send()
            relay(step, rows, other).wait_send()
            return carry

        lax.fori_loop(1, n // 2, sent, 0)
    over(lambda d: when(d < red, lambda: scatter(d, me).wait_send()))
    when(me < red, lambda: over(lambda d: gather(d, me).wait_send()))
    over(lambda d: final(d, me).wait_send())


def shards(
    rhs,
    near_blocks,
    near_nbrs,
    row_basis,
    col_basis,
    couplings,
    far_owner,
    far_slot,
    leaf_perm,
    leaf_size,
):
    n = lax.axis_size("leaf")
    vmem = pl.BlockSpec(memory_space=pltpu.VMEM)
    anyspace = pl.BlockSpec(memory_space=pltpu.HBM)
    dma = pltpu.SemaphoreType.DMA
    return pl.pallas_call(
        functools.partial(kernel, n),
        out_shape=jax.ShapeDtypeStruct((R, LD, M), F32),
        in_specs=[anyspace] * 10,
        out_specs=vmem,
        scratch_shapes=[
            pltpu.SMEM((LD, NB), jnp.int32),
            pltpu.SMEM((LD,), jnp.int32),
            pltpu.VMEM((R, LD, M), F32),
            pltpu.VMEM((LD, M), jnp.int32),
            pltpu.VMEM((LD, K, M), F32),
            pltpu.VMEM((LD, K, M), F32),
            pltpu.VMEM((K, K, M), F32),
            pltpu.VMEM((1, M), jnp.int32),
            pltpu.VMEM((1, M), jnp.int32),
            pltpu.VMEM((LD, NB, M, M), F32),
            pltpu.VMEM((LD, M, NB * M), BF16),
            pltpu.VMEM((LD, M, NB * M), BF16),
            pltpu.VMEM((n, M, M), BF16),
            pltpu.VMEM((n, M, M), BF16),
            pltpu.VMEM((LD, M, M), BF16),
            pltpu.VMEM((LD, M, M), BF16),
            pltpu.VMEM((LD, M, M), BF16),
            pltpu.VMEM((LD, M, M), BF16),
            pltpu.VMEM((LD, M, M), F32),
            pltpu.VMEM((ITERS, 2, LD, R, M), F32),
            pltpu.VMEM((3 * LD, 2 * R, M), BF16),
            pltpu.VMEM((ITERS, n, R + 8, M), F32),
            pltpu.VMEM((SPAN, CHUNK, M), F32),
            pltpu.VMEM((n, CHUNK, M), F32),
            pltpu.VMEM((SPAN, CHUNK, M), F32),
            pltpu.VMEM((n, R, M), F32),
            pltpu.VMEM((M, M), F32),
            dma((9,)),
            dma((LD,)),
            dma((ITERS, 2)),
            dma((ITERS, 2)),
            dma((ITERS, n)),
            dma((ITERS, n)),
            dma((ITERS, n)),
            dma((n,)),
            dma((n,)),
            dma((n,)),
            dma((n,)),
            dma((n,)),
            dma((n,)),
        ],
        compiler_params=pltpu.CompilerParams(
            collective_id=0, has_side_effects=True, vmem_limit_bytes=56 * 1024 * 1024
        ),
    )(
        near_blocks,
        near_nbrs,
        leaf_size,
        rhs,
        leaf_perm,
        jnp.swapaxes(row_basis, 1, 2),
        jnp.swapaxes(col_basis, 1, 2),
        jnp.transpose(couplings, (1, 2, 0)),
        far_owner.reshape(1, -1),
        far_slot.reshape(1, -1),
    )


def solution(mesh):
    in_specs = (
        P(None, ("grp", "leaf"), None),
        P(("grp", "leaf"), None, None, None),
        P(("grp", "leaf"), None),
        P(("grp", "leaf"), None, None),
        P(("grp", "leaf"), None, None),
        P(("grp", "leaf"), None, None),
        P(("grp", "leaf"), None),
        P(("grp", "leaf")),
        P(("grp", "leaf"), None),
        P(("grp", "leaf")),
    )
    out_specs = P(None, ("grp", "leaf"), None)
    return jax.shard_map(shards, mesh=mesh, in_specs=in_specs, out_specs=out_specs, check_vma=False)
```
